512 devices in a mesh: rep: 8 (over y, z_hi), fsdp: 64 (over x, z_lo, core).
Axes of the slice: x: 4, y: 4, z: 16 (z_hi: 2, z_lo: 8; z = z_hi * 8 + z_lo), core: 2. Of those that a mesh axis runs over, the one named last changes fastest.
Arguments:
- tokens: bfloat16 [131072, 4096], P(('rep', 'fsdp')), may hold values from -24 to 24
- queries: bfloat16 [131072, 2048], P(('rep', 'fsdp')), may hold values from -182 to 182
- key_vectors: bfloat16 [131072, 256], P(('rep', 'fsdp')), may hold values from -5 to 5
- cotangent: bfloat16 [131072, 2048], P(('rep', 'fsdp')), may hold values from -0.1875 to 0.1875
- positions: int32 [131072], P(('rep', 'fsdp')), may hold values from 0 to 4351, as said below
- doc_ids: int32 [131072], P(('rep', 'fsdp')), may hold values from 0 to 254, as said below
- weight: float32 [4096, 256], P('fsdp'), may hold values from -0.09375 to 0.09375
- moment_one: float32 [4096, 256], P('fsdp'), may hold values from -16 to 16
- moment_two: float32 [4096, 256], P('fsdp'), may hold values from 1 to 100
- old_ids: int32 [64], replicated, may hold values from 0 to 63, each once
- new_ids: int32 [64], replicated, may hold values from 0 to 31, as said below
Outputs:
- new_weight: float32 [8192, 256], P('fsdp')
- new_moment_one: float32 [8192, 256], P('fsdp')
- new_moment_two: float32 [8192, 256], P('fsdp')
- token_loss: float32 [131072], P(('rep', 'fsdp'))
The draws below stay inside these ranges and needn't reach their ends.
Inputs may be any that keep to these rules, and one draw needn't show every extreme that they name: `new_ids`: each new shard number is held by exactly two indices. `doc_ids`: along each sequence of 256 tokens the numbers start at 0 and never fall. Within one document of a sequence, positions rise by one from token to token.
All inputs are finite; a program needn't handle non-finite values.
Results may differ from the reference program's by a relative error of at most 0.008.
Values may be sent and summed in bfloat16 or wider, within the bound.
A program may use at most 64 MiB of HBM per device.

```python
import math
import jax
import jax.numpy as jnp
from jax import lax

D = 4096
HEADS = 32
KV_HEADS = 4
HEAD_DIM = 64
TOK_DEV = 256
KV_COLS = 256
TOKENS = 131072
N_FSDP = 64


def layout_draw(key):
    sequences = TOKENS // TOK_DEV
    token_index = jnp.arange(TOK_DEV, dtype=jnp.int32)
    aligned = jax.random.randint(jax.random.fold_in(key, 101), (sequences,), 1, TOK_DEV)
    starts = jax.random.randint(jax.random.fold_in(key, 102), (sequences, TOK_DEV), 0, max(TOK_DEV // 3, 2)) == 0
    dense_row = (jnp.arange(sequences, dtype=jnp.int32) == sequences - 1)[:, None]
    starts = (starts | dense_row) & (token_index[None, :] != aligned[:, None]) | (token_index[None, :] == 0)
    doc_number = jnp.cumsum(starts.astype(jnp.int32), axis=1) - 1
    first_index = lax.cummax(jnp.where(starts, token_index[None, :], 0), axis=1)
    offsets = jax.random.randint(jax.random.fold_in(key, 103), (sequences, TOK_DEV), 0, 4096)
    first_row = (jnp.arange(sequences, dtype=jnp.int32) == 0)[:, None]
    offsets = jnp.where(first_row, 4096 + token_index[None, :], offsets)
    places = jnp.take_along_axis(offsets, first_index, axis=1) + token_index[None, :] - first_index
    return (doc_number, places)


def draw_doc_ids(key, part):
    return layout_draw(key)[0].reshape(TOKENS)


def draw_positions(key, part):
    return layout_draw(key)[1].reshape(TOKENS)


def draw_new_ids(key, part):
    return jax.random.permutation(jax.random.fold_in(key, 104), jnp.arange(N_FSDP, dtype=jnp.int32) // 2)


def draw_queries(key, part):
    sequences = TOKENS // TOK_DEV
    drawn_rows = jax.random.truncated_normal(jax.random.fold_in(key, 201), -4.0, 4.0, (sequences, TOK_DEV, HEADS, HEAD_DIM), jnp.float32)
    return drawn_rows.reshape(TOKENS, HEADS * HEAD_DIM).astype(jnp.bfloat16)


def draw_key_vectors(key, part):
    sequences = TOKENS // TOK_DEV
    drawn_rows = jax.random.truncated_normal(jax.random.fold_in(key, 202), -4.0, 4.0, (sequences, TOK_DEV, KV_HEADS, HEAD_DIM), jnp.float32)
    return drawn_rows.reshape(TOKENS, KV_HEADS * HEAD_DIM).astype(jnp.bfloat16)


def spiked(values, key, source, target, parts, factor):
    owner, partner = [(jnp.arange(values.shape[position]) // (values.shape[position] // parts)).reshape([-1 if axis == position else 1 for axis in range(values.ndim)]) for position in (source, target)]
    chosen = jax.random.permutation(key, parts)[partner]
    strong = (owner == chosen) | (owner == (partner + parts // 2) % parts)
    return jnp.where(strong, factor * values, values)


def level_of(own_key, dims, cuts, smallest, largest):
    factor_of = 1.0
    for axis_at, parts in cuts:
        draws = jax.random.uniform(jax.random.fold_in(jax.random.fold_in(own_key, 6), axis_at), (parts,), jnp.float32, smallest / len(cuts), largest / len(cuts))
        factor_of = factor_of * jnp.repeat(jnp.exp(draws), dims[axis_at] // parts).reshape((-1,) + (1,) * (len(dims) - 1 - axis_at))
    return factor_of


def normal_values(stream_key, extent, scale, bound, cuts=(), kind=jnp.bfloat16):
    gain = level_of(stream_key, extent, cuts, -0.22, 0.18) if cuts else 1.0
    result = jax.random.normal(stream_key, extent, jnp.float32) * scale * gain
    return jnp.minimum(jnp.maximum(result, -bound), bound).astype(kind)


def noise_with(key, shape, scale, limit, shards, heavy, kind=jnp.bfloat16):
    array = scale * jax.random.normal(key, shape, jnp.float32)
    if shards:
        array = array * level_of(key, shape, shards, -0.22, 0.18)
    return jnp.clip(spiked(array, jax.random.fold_in(key, 3), *heavy), -limit, limit).astype(kind)


def setup_inputs(seed: int = 0) -> dict:
    splits = jax.random.split(jax.random.key(seed), 12)
    return {
        "tokens": noise_with(splits[0], (TOKENS, D), 1.0, 24.0, ((0, 512),), (0, 1, 512, 6.0)),
        "queries": draw_queries(jax.random.fold_in(splits[11], 71), 0),
        "key_vectors": draw_key_vectors(jax.random.fold_in(splits[11], 71), 0),
        "cotangent": normal_values(splits[3], (TOKENS, HEADS * HEAD_DIM), 0.03, 0.1875, ((0, 512),)),
        "positions": draw_positions(jax.random.fold_in(splits[11], 71), 0),
        "doc_ids": draw_doc_ids(jax.random.fold_in(splits[11], 71), 0),
        "weight": normal_values(splits[6], (D, KV_COLS), D ** -0.5, 0.09375, ((0, 64),), jnp.float32),
        "moment_one": normal_values(splits[7], (D, KV_COLS), 3.0, 16.0, ((0, 64),), jnp.float32),
        "moment_two": jnp.clip(jnp.exp(math.log(100.0) - 4.6051702 * jax.random.uniform(splits[8], (D, KV_COLS), jnp.float32) ** level_of(splits[8], (D, KV_COLS), ((0, 64),), -0.2, 0.2)), 1.0, 100.0),
        "old_ids": jax.random.permutation(splits[9], N_FSDP).astype(jnp.int32),
        "new_ids": draw_new_ids(jax.random.fold_in(splits[11], 71), 0),
    }


rope_base = 500000.0
learn_rate = 0.0003 * math.sqrt(2.0)
beta_one = 0.9
beta_two = 0.95
adam_eps = 1e-08
decay_rate = 0.1
step_count = 40

def rotate(values, places):
    half_dim = values.shape[-1] // 2
    frequency = rope_base ** (-(jnp.arange(half_dim, dtype=jnp.float32) * 2.0 / values.shape[-1]))
    angles = places.astype(jnp.float32)[:, None] * frequency[None, :]
    target_shape = (angles.shape[0],) + (1,) * (values.ndim - 2) + (half_dim,)
    cosine = jnp.cos(angles).reshape(target_shape)
    sine_part = jnp.sin(angles).reshape(target_shape)
    first_part = values[..., :half_dim]
    second_part = values[..., half_dim:]
    return jnp.concatenate([first_part * cosine - second_part * sine_part, second_part * cosine + first_part * sine_part], axis=-1)

def adam_step(weight, moment_one, moment_two, gradient):
    moment_new = beta_one * moment_one + (1.0 - beta_one) * gradient
    second_new = beta_two * moment_two + (1.0 - beta_two) * gradient * gradient
    first_fix = 1.0 - beta_one ** step_count
    second_fix = 1.0 - beta_two ** step_count
    update = moment_new / first_fix / (jnp.sqrt(second_new / second_fix) + adam_eps)
    weight_new = weight - learn_rate * (update + decay_rate * weight)
    return (weight_new, moment_new, second_new)

def reference(tokens, queries, key_vectors, cotangent, positions, doc_ids, weight, moment_one, moment_two, old_ids, new_ids):
    shard_rows = D // N_FSDP
    kv_cols = KV_HEADS * HEAD_DIM
    group_size = HEADS // KV_HEADS
    sequences = TOKENS // TOK_DEV
    inverse = jnp.zeros((N_FSDP,), jnp.int32).at[old_ids].set(jnp.arange(N_FSDP, dtype=jnp.int32))

    def unshard(stacked):
        return stacked.reshape(N_FSDP, shard_rows, kv_cols)[inverse].reshape(D, kv_cols)
    full_weight = unshard(weight)
    first_full = unshard(moment_one)
    second_full = unshard(moment_two)
    weight_low = full_weight.astype(jnp.bfloat16)
    token_index = jnp.arange(TOK_DEV, dtype=jnp.int32)

    def one_sequence(gradient, inputs):
        token_rows, query_rows, key_rows, upstream, place_rows, doc_rows = inputs
        values = jnp.dot(token_rows, weight_low, preferred_element_type=jnp.float32).astype(jnp.bfloat16)
        values = values.reshape(TOK_DEV, KV_HEADS, HEAD_DIM)
        query_rot = rotate(query_rows.astype(jnp.float32).reshape(TOK_DEV, KV_HEADS, group_size, HEAD_DIM), place_rows).astype(jnp.bfloat16)
        key_rot = rotate(key_rows.astype(jnp.float32).reshape(TOK_DEV, KV_HEADS, HEAD_DIM), place_rows).astype(jnp.bfloat16)
        scores = jnp.einsum('tkgd,ukd->kgtu', query_rot.astype(jnp.float32), key_rot.astype(jnp.float32)) / math.sqrt(HEAD_DIM)
        allowed = (token_index[None, :] <= token_index[:, None]) & (doc_rows[None, :] == doc_rows[:, None])
        scores = jnp.where(allowed[None, None], scores, -1e+30)
        row_peak = lax.optimization_barrier(jnp.max(scores, axis=-1, keepdims=True))
        raised = jnp.exp(scores - row_peak)
        attention_probs = raised / lax.optimization_barrier(jnp.sum(raised, axis=-1, keepdims=True))
        rounded_probs = attention_probs.astype(jnp.bfloat16)
        mixed_out = jnp.einsum('kgtu,ukd->tkgd', rounded_probs.astype(jnp.float32), values.astype(jnp.float32))
        upstream_rows = upstream.reshape(TOK_DEV, KV_HEADS, group_size, HEAD_DIM).astype(jnp.float32)
        token_loss = lax.optimization_barrier(jnp.sum(mixed_out * upstream_rows, axis=(1, 2, 3)))
        value_grad = jnp.einsum('kgtu,tkgd->ukd', rounded_probs.astype(jnp.float32), upstream_rows)
        value_grad = value_grad.astype(jnp.bfloat16).reshape(TOK_DEV, kv_cols)
        gradient = gradient + jnp.dot(token_rows.T, value_grad, preferred_element_type=jnp.float32)
        return (gradient, token_loss)
    inputs = (tokens.reshape(sequences, TOK_DEV, D), queries.reshape(sequences, TOK_DEV, HEADS * HEAD_DIM), key_vectors.reshape(sequences, TOK_DEV, kv_cols), cotangent.reshape(sequences, TOK_DEV, HEADS * HEAD_DIM), positions.reshape(sequences, TOK_DEV), doc_ids.reshape(sequences, TOK_DEV))
    gradient, losses = lax.scan(one_sequence, jnp.zeros((D, kv_cols), jnp.float32), inputs)
    weight_new, moment_new, second_new = adam_step(full_weight, first_full, second_full, gradient)

    def reshard(stacked):
        return stacked.reshape(N_FSDP // 2, 2 * shard_rows, kv_cols)[new_ids].reshape(N_FSDP * 2 * shard_rows, kv_cols)
    return (reshard(weight_new), reshard(moment_new), reshard(second_new), losses.reshape(TOKENS))
```

```python
import functools
import math

import jax
import jax.numpy as jnp
from jax import lax
from jax.experimental import pallas as pl
from jax.experimental.pallas import tpu as pltpu
from jax.sharding import PartitionSpec as P

MESH = pl.DeviceIdType.MESH
BF = jnp.bfloat16
F32 = jnp.float32

rope_base = 500000.0
learn_rate = 0.0003 * math.sqrt(2.0)
beta_one = 0.9
beta_two = 0.95
adam_eps = 1e-08
decay_rate = 0.1
step_count = 40

TOK = 256
NB = 32
GROUP = [(dq, dc) for dq in range(4) for dc in range(2) if (dq, dc) != (0, 0)]
Z_OFFS = [-3, -2, -1, 1, 2, 3, 4]


def adam_step(weight, moment_one, moment_two, gradient):
    moment_new = beta_one * moment_one + (1.0 - beta_one) * gradient
    second_new = beta_two * moment_two + (1.0 - beta_two) * gradient * gradient
    first_fix = 1.0 - beta_one**step_count
    second_fix = 1.0 - beta_two**step_count
    update = moment_new / first_fix / (jnp.sqrt(second_new / second_fix) + adam_eps)
    weight_new = weight - learn_rate * (update + decay_rate * weight)
    return (weight_new, moment_new, second_new)


def portion_scratch():
    return dict(
        part=pltpu.VMEM((8, NB, 16, 128), BF),
        core_in=pltpu.VMEM((4, NB, 16, 128), BF),
        q1_out=pltpu.VMEM((3, NB, 16, 128), BF),
        q1_in=pltpu.VMEM((3, NB, 16, 128), BF),
        q2_sum=pltpu.VMEM((NB, 16, 128), F32),
        q2_out=pltpu.VMEM((NB, 16, 128), BF),
        q2_in=pltpu.VMEM((3, 8, 16, 128), BF),
        za_sum=pltpu.VMEM((8, 16, 128), F32),
        za_out=pltpu.VMEM((8, 16, 128), BF),
        za_in=pltpu.VMEM((3, 2, 16, 128), BF),
        zb_sum=pltpu.VMEM((2, 16, 128), F32),
        zb_out=pltpu.VMEM((2, 16, 128), BF),
        zb_in=pltpu.VMEM((3, 16, 128), BF),
        full=pltpu.VMEM((NB, 16, 128), BF),
        pick=pltpu.VMEM((7, 16, 128), BF),
        mine=pltpu.VMEM((8, 16, 128), BF),
    )


def scratch_plan():
    plan = dict(
        state_out=pltpu.VMEM((8, 16, 128), BF),
        moments_out=pltpu.VMEM((8, 32, 128), BF),
        wall=pltpu.VMEM((8, 8, 8, 16, 128), BF),
        mv=pltpu.VMEM((8, 8, 32, 128), BF),
        mv_pick=pltpu.VMEM((7, 2, 32, 128), BF),
        mv_in=pltpu.VMEM((8, 2, 32, 128), BF),
        wnat=pltpu.VMEM((4096, 256), BF),
        probs=pltpu.VMEM((16, 512, 256), BF),
        keys2=pltpu.VMEM((4, 512, 128), BF),
        vals2=pltpu.VMEM((4, 512, 128), BF),
        bias=pltpu.VMEM((256, 256), F32),
        dacc=pltpu.VMEM((2, 2, 256, 128), F32),
        lacc=pltpu.VMEM((8, 256), F32),
        vacc=pltpu.VMEM((256, 256), F32),
    )
    for name in "ab":
        for key, value in portion_scratch().items():
            plan[name + "_" + key] = value
    plan["send"] = pltpu.SemaphoreType.DMA((128,))
    plan["recv"] = pltpu.SemaphoreType.DMA((128,))
    return plan


PLAN = scratch_plan()


def doubled(pair, odd):
    lane = lax.broadcasted_iota(jnp.int32, pair.shape, 1)
    turned = pltpu.roll(pair, 64, 1)
    low, high = (turned, pair) if odd else (pair, turned)
    top = jnp.where(lane < 64, low, 0.0)
    bottom = jnp.where(lane >= 64, high, 0.0)
    return jnp.concatenate([top, bottom], axis=0)


def kernel(
    inv_ref, new_ref, tok_ref, q_ref, k_ref, cot_ref, trig_ref, doc_ref, w_ref, m_ref, v_ref,
    wo_ref, mo_ref, vo_ref, loss_ref, *scratch
):
    s = dict(zip(PLAN, scratch))
    send, recv = s["send"], s["recv"]
    rep = lax.axis_index("rep")
    fs = lax.axis_index("fsdp")
    y = rep // 2
    x = fs // 16
    zl = (fs // 2) % 8
    core = fs % 2
    z = (rep % 2) * 8 + zl
    a, b = z // 4, z % 4
    me_c = x * 2 + core

    def dev(dx=0, dy=0, dz=0, dc=0):
        nx, ny, nz, nc = (x + dx) % 4, (y + dy) % 4, (z + dz + 16) % 16, (core + dc) % 2
        return (ny * 2 + nz // 8, (nx * 8 + nz % 8) * 2 + nc)

    used = [0]
    pending = []

    def copy(src, dst, where):
        idx = used[0]
        used[0] += 1
        made = pltpu.make_async_remote_copy(
            src_ref=src, dst_ref=dst, send_sem=send.at[idx], recv_sem=recv.at[idx],
            device_id=where, device_id_type=MESH,
        )
        made.start()
        pending.append(made)
        return made

    def arrive(copies):
        for made in copies:
            made.wait_recv()

    barrier = pltpu.get_barrier_semaphore()
    partners = [dict(dx=dq, dc=dc) for dq, dc in GROUP]
    partners += [dict(dy=dq, dc=dc) for dq, dc in GROUP if dq]
    partners += [dict(dz=dz) for dz in (-4, -3, -2, -1, 1, 2, 3, 4, 8)]
    for partner in partners:
        pl.semaphore_signal(barrier, inc=1, device_id=dev(**partner), device_id_type=MESH)

    for c in range(8):
        rows, cols = pl.ds(16 * (c // 2), 16), pl.ds(128 * (c % 2), 128)
        s["state_out"][c] = w_ref[rows, cols].astype(BF)
        s["moments_out"][c, 0:16] = m_ref[rows, cols].astype(BF)
        s["moments_out"][c, 16:32] = v_ref[rows, cols].astype(BF)
    s["wall"][me_c, 3, me_c] = s["state_out"][me_c]
    s["mv"][3, me_c] = s["moments_out"][me_c]
    pl.semaphore_wait(barrier, len(partners))

    first = []
    for dq, dc in GROUP:
        to_c = ((x + dq) % 4) * 2 + (core + dc) % 2
        first.append(copy(s["state_out"].at[to_c], s["wall"].at[to_c, 3, me_c], dev(dx=dq, dc=dc)))
        first.append(copy(s["moments_out"].at[to_c], s["mv"].at[3, me_c], dev(dx=dq, dc=dc)))

    lane128 = lax.broadcasted_iota(jnp.int32, (TOK, 128), 1)
    low_half = (lane128 % 64) < 32

    def rotated(pair):
        swapped = jnp.where(low_half, pltpu.roll(pair, 96, 1), pltpu.roll(pair, 32, 1))
        return pair * trig_ref[:, 0:128] + swapped * trig_ref[:, 128:256]

    for i in range(2):
        turned = rotated(k_ref[:, 128 * i:128 * i + 128].astype(F32))
        for odd in range(2):
            s["keys2"][2 * i + odd] = doubled(turned, odd).astype(BF)
    docs = doc_ref[...].astype(F32)
    columns = jnp.transpose(jnp.broadcast_to(docs, (128, TOK)))
    own_row = lax.broadcasted_iota(jnp.int32, (TOK, 128), 0)
    for half in range(2):
        allowed = (own_row <= lane128 + 128 * half) & (columns == docs[:, 128 * half:128 * half + 128])
        s["bias"][:, 128 * half:128 * half + 128] = jnp.where(allowed, 0.0, -1e30)

    def attention(g):
        def pair_step(i, _):
            q = 4 * g + i
            cols = pl.ds(pl.multiple_of(q * 128, 128), 128)
            rq = rotated(q_ref[:, cols].astype(F32)).astype(BF)
            cot = cot_ref[:, cols]
            for odd in range(2):
                scores = lax.dot_general(
                    s["keys2"][g, 256 * odd:256 * odd + 256, :], rq, (((1,), (1,)), ((), ())),
                    preferred_element_type=F32,
                )
                scores = scores * 0.125 + s["bias"][...]
                raised = jnp.exp(scores - jnp.max(scores, axis=0, keepdims=True))
                probs = (raised * (1.0 / jnp.sum(raised, axis=0, keepdims=True))).astype(BF)
                s["probs"][q, 256 * odd:256 * odd + 256, :] = probs
                s["dacc"][g % 2, odd] += jnp.dot(probs, cot, preferred_element_type=F32)
            return 0

        s["dacc"][g % 2] = jnp.zeros((2, 256, 128), F32)
        lax.fori_loop(0, 4, pair_step, 0)

    def partial(name):
        d = s["dacc"]
        low = d[0, 0] + pltpu.roll(d[0, 1], 64, 1)
        high = pltpu.roll(d[1, 0], 64, 1) + d[1, 1]
        grad = jnp.where(lane128 < 64, low, high)
        turned = jnp.transpose(grad).astype(BF)
        out = s[name + "_part"]

        def block(i, _):
            r = jnp.dot(turned, tok_ref[:, pl.ds(pl.multiple_of(i * 512, 512), 512)], preferred_element_type=F32)
            r = r.astype(BF)
            for k in range(4):
                for p in range(8):
                    out[p, 4 * i + k] = r[16 * p:16 * p + 16, 128 * k:128 * k + 128]
            return 0

        lax.fori_loop(0, 8, block, 0)

    def f(value):
        return value.astype(F32)

    def over(n, step, body):
        def run(i, _):
            body(pl.ds(i * step, step))
            return 0

        lax.fori_loop(0, n // step, run, 0)

    class Portion:
        def __init__(self, name):
            self.name = name
            self.q1, self.q2 = (x, y) if name == "a" else (y, x)

        def buf(self, key):
            return s[self.name + "_" + key]

        def at1(self, r, dc=0):
            return dev(dx=r, dc=dc) if self.name == "a" else dev(dy=r, dc=dc)

        def at2(self, r):
            return dev(dy=r) if self.name == "a" else dev(dx=r)

        def send_core(self):
            self.c0 = [copy(self.buf("part").at[pl.ds(4 * (1 - core), 4)], self.buf("core_in"), dev(dc=1))]

        def send_q1(self):
            arrive(self.c0)
            part, came, out = self.buf("part"), self.buf("core_in"), self.buf("q1_out")
            self.c1 = []
            for r in (2, 1, 3):
                to = (self.q1 + r) % 4

                def add(n):
                    out[r - 1, n] = (f(part[core * 4 + to, n]) + f(came[to, n])).astype(BF)

                over(NB, 4, add)
                self.c1.append(copy(out.at[r - 1], self.buf("q1_in").at[r - 1], self.at1(r)))

        def send_q2(self):
            arrive(self.c1)
            part, came, got = self.buf("part"), self.buf("core_in"), self.buf("q1_in")
            total, out = self.buf("q2_sum"), self.buf("q2_out")

            def add(n):
                t = f(part[core * 4 + self.q1, n]) + f(came[self.q1, n])
                t = t + f(got[0, n]) + f(got[1, n]) + f(got[2, n])
                total[n] = t
                out[n] = t.astype(BF)

            over(NB, 4, add)
            self.c2 = []
            for r in (2, 1, 3):
                to = (self.q2 + r) % 4
                self.c2.append(copy(out.at[pl.ds(8 * to, 8)], self.buf("q2_in").at[r - 1], self.at2(r)))

        def send_za(self):
            arrive(self.c2)
            got, total, out = self.buf("q2_in"), self.buf("za_sum"), self.buf("za_out")
            t = self.buf("q2_sum")[pl.ds(8 * self.q2, 8)]
            t = t + f(got[0]) + f(got[1]) + f(got[2])
            total[...] = t
            out[...] = t.astype(BF)
            self.c3 = []
            for r in (2, 1, 3):
                to = (b + r) % 4
                self.c3.append(copy(out.at[pl.ds(2 * to, 2)], self.buf("za_in").at[r - 1], dev(dz=to - b)))

        def send_zb(self):
            arrive(self.c3)
            got, total, out = self.buf("za_in"), self.buf("zb_sum"), self.buf("zb_out")
            t = self.buf("za_sum")[pl.ds(2 * b, 2)] + f(got[0]) + f(got[1]) + f(got[2])
            total[...] = t
            out[...] = t.astype(BF)
            self.c4 = []
            for r in (2, 1, 3):
                self.c4.append(copy(out.at[(a + r) % 2], self.buf("zb_in").at[r - 1], dev(dz=4 * r)))

        def gather_z(self):
            arrive(self.c4)
            got, full = self.buf("zb_in"), self.buf("full")
            slot = 8 * self.q2 + 2 * b + a % 2
            t = self.buf("zb_sum")[a % 2] + f(got[0]) + f(got[1]) + f(got[2])
            full[slot] = t.astype(BF)
            self.c5 = [copy(full.at[slot], full.at[slot], dev(dz=o)) for o in Z_OFFS]

        def gather_q2(self):
            arrive(self.c5)
            full = self.buf("full")
            own = pl.ds(8 * self.q2, 8)
            self.c6 = [copy(full.at[own], full.at[own], self.at2(r)) for r in (2, 1, 3)]

        def exchange(self):
            arrive(self.c6)
            full, pick, mine = self.buf("full"), self.buf("pick"), self.buf("mine")
            piece = core * 4 + self.q1
            self.c7 = []
            for idx, (dq, dc) in enumerate(GROUP):
                to_x = (x + dq) % 4 if self.name == "a" else x
                pick[idx] = full[new_ref[(to_x * 8 + zl) * 2 + (core + dc) % 2]]
                self.c7.append(copy(pick.at[idx], mine.at[piece], self.at1(dq, dc)))
            mine[piece] = full[new_ref[fs]]

        def gradient(self):
            arrive(self.c7)
            return jnp.transpose(f(self.buf("mine")[...]).reshape(128, 128))

    pa, pb = Portion("a"), Portion("b")
    wall, mv = s["wall"], s["mv"]

    def z_step(step):
        out = []
        up, down = 3 + (step - 1), 3 - (step - 1)
        if step < 4:
            pairs = [(up, up + 1, -1, pl.ds(0, 8)), (down, down - 1, 1, pl.ds(0, 8))]
        else:
            pairs = [(6, 7, -1, pl.ds(0, 4)), (0, 7, 1, pl.ds(4, 4))]
        for src, dst, dz, part in pairs:
            out.append(copy(wall.at[me_c, src, part], wall.at[me_c, dst, part], dev(dz=dz)))
            out.append(copy(mv.at[src, part], mv.at[dst, part], dev(dz=dz)))
        return out

    def where(j):
        return ((j // 2) % 8 - zl + 11) % 8, (j // 16) * 2 + j % 2

    attention(0)
    arrive(first)
    ring = z_step(1)
    attention(1)
    partial("a")
    pa.send_core()
    arrive(ring)
    ring = z_step(2)
    attention(2)
    pa.send_q1()
    arrive(ring)
    ring = z_step(3)
    attention(3)
    partial("b")
    pb.send_core()
    arrive(ring)
    ring = z_step(4)
    pa.send_q2()
    pb.send_q1()
    pa.send_za()
    arrive(ring)

    moved = []
    for idx, (dq, dc) in enumerate(GROUP):
        n = new_ref[(((x + dq) % 4) * 8 + zl) * 2 + (core + dc) % 2]
        for i in range(2):
            slot, c = where(inv_ref[2 * n + i])
            s["mv_pick"][idx, i] = mv[slot, c]
        moved.append(copy(s["mv_pick"].at[idx], s["mv_in"].at[me_c], dev(dx=dq, dc=dc)))
    own_n = new_ref[fs]
    for i in range(2):
        slot, c = where(inv_ref[2 * own_n + i])
        s["mv_in"][me_c, i] = mv[slot, c]
    def wcopy(c, part, where_to):
        return copy(wall.at[c, part], wall.at[c, part], where_to)

    all_z = pl.ds(0, 8)
    left_c, right_c = ((x + 3) % 4) * 2 + core, ((x + 1) % 4) * 2 + core
    far_c = ((x + 2) % 4) * 2 + core
    along_x = [wcopy(me_c, all_z, dev(dx=1)), wcopy(me_c, all_z, dev(dx=3))]
    across = [wcopy(me_c, all_z, dev(dc=1))]
    pa.send_zb()
    pb.send_q2()
    pa.gather_z()
    pb.send_za()
    arrive(along_x)
    far = [wcopy(left_c, pl.ds(0, 4), dev(dx=1)), wcopy(right_c, pl.ds(4, 4), dev(dx=3))]
    across += [wcopy(left_c, all_z, dev(dc=1)), wcopy(right_c, all_z, dev(dc=1))]
    pa.gather_q2()
    pb.send_zb()
    pa.exchange()
    pb.gather_z()
    arrive(far)
    across.append(wcopy(far_c, all_z, dev(dc=1)))
    pb.gather_q2()
    arrive(across)

    wnat = s["wnat"]

    def natural(i, _):
        slot, c = where(inv_ref[i])
        base = pl.multiple_of(i * 64, 64)
        for piece in range(8):
            wnat[pl.ds(base + 16 * (piece // 2), 16), 128 * (piece % 2):128 * (piece % 2) + 128] = wall[piece, slot, c]
        return 0

    lax.fori_loop(0, 64, natural, 0)
    pb.exchange()
    s["vacc"][...] = jnp.zeros((256, 256), F32)

    def project(i, _):
        k = pl.ds(pl.multiple_of(i * 512, 512), 512)
        s["vacc"][...] += jnp.dot(tok_ref[:, k], wnat[k, :], preferred_element_type=F32)
        return 0

    lax.fori_loop(0, 8, project, 0)
    for i in range(2):
        pair = s["vacc"][:, 128 * i:128 * i + 128]
        for odd in range(2):
            s["vals2"][2 * i + odd] = doubled(pair, odd).astype(BF)
    s["lacc"][...] = jnp.zeros((8, 256), F32)

    def loss_step(q, _):
        cot = cot_ref[:, pl.ds(pl.multiple_of(q * 128, 128), 128)]
        g = q // 4
        t = lax.dot_general(s["vals2"][g], cot, (((1,), (1,)), ((), ())), preferred_element_type=F32)
        t = t * f(s["probs"][q])
        s["lacc"][...] += jnp.sum(t.reshape(64, 8, 256), axis=0)
        return 0

    lax.fori_loop(0, 16, loss_step, 0)
    loss_ref[...] = jnp.sum(s["lacc"][...], axis=0, keepdims=True)

    arrive(moved)
    grads = [pa.gradient(), pb.gradient()]
    for i in range(2):
        slot, src = where(inv_ref[2 * own_n + i])
        for c in range(8):
            r0, l0 = 64 * i + 16 * (c // 2), 128 * (c % 2)
            weight = f(wall[c, slot, src])
            one = f(s["mv_in"][c, i, 0:16])
            two = f(s["mv_in"][c, i, 16:32])
            new = adam_step(weight, one, two, grads[c % 2][r0:r0 + 16])
            for ref, value in zip((wo_ref, mo_ref, vo_ref), new):
                ref[r0:r0 + 16, l0:l0 + 128] = value
    for made in pending:
        made.wait_send()


def shards(
    tokens, queries, key_vectors, cotangent, positions, doc_ids, weight, moment_one, moment_two, old_ids, new_ids
):
    index = jnp.arange(64, dtype=jnp.int32)
    inverse = jnp.sum(jnp.where(old_ids[None, :] == index[:, None], index[None, :], 0), axis=1)
    lane = jnp.arange(256, dtype=jnp.int32)
    half = (lane % 32).astype(F32)
    frequency = rope_base ** (-(half * 2.0 / 64))
    angles = positions.astype(F32)[:, None] * frequency[None, :]
    signed = jnp.where((lane % 64) < 32, -jnp.sin(angles), jnp.sin(angles))
    trig = jnp.where(lane < 128, jnp.cos(angles), signed)

    vmem = pl.BlockSpec(memory_space=pltpu.VMEM)
    smem = pl.BlockSpec(memory_space=pltpu.SMEM)
    outs = pl.pallas_call(
        kernel,
        out_shape=[jax.ShapeDtypeStruct((128, 256), F32)] * 3 + [jax.ShapeDtypeStruct((1, 256), F32)],
        in_specs=[smem, smem] + [vmem] * 9,
        out_specs=[vmem] * 4,
        scratch_shapes=list(PLAN.values()),
        compiler_params=pltpu.CompilerParams(
            collective_id=0, has_side_effects=True, vmem_limit_bytes=48 * 1024 * 1024
        ),
        cost_estimate=pl.CostEstimate(flops=2_200_000_000, bytes_accessed=6_000_000, transcendentals=2_200_000),
    )(
        inverse, new_ids, tokens, queries, key_vectors, cotangent, trig, doc_ids.reshape(1, 256),
        weight, moment_one, moment_two,
    )
    return (outs[0], outs[1], outs[2], outs[3].reshape(256))


def solution(mesh):
    in_specs = (
        P(("rep", "fsdp"), None),
        P(("rep", "fsdp"), None),
        P(("rep", "fsdp"), None),
        P(("rep", "fsdp"), None),
        P(("rep", "fsdp")),
        P(("rep", "fsdp")),
        P("fsdp", None),
        P("fsdp", None),
        P("fsdp", None),
        P(),
        P(),
    )
    out_specs = (P("fsdp", None), P("fsdp", None), P("fsdp", None), P(("rep", "fsdp")))
    return jax.shard_map(shards, mesh=mesh, in_specs=in_specs, out_specs=out_specs, check_vma=False)
```

```python
import math

import jax
import jax.numpy as jnp
from jax import lax
from jax.experimental import pallas as pl
from jax.experimental.pallas import tpu as pltpu
from jax.sharding import PartitionSpec as P

MESH = pl.DeviceIdType.MESH
BF = jnp.bfloat16
F32 = jnp.float32

rope_base = 500000.0
learn_rate = 0.0003 * math.sqrt(2.0)
beta_one = 0.9
beta_two = 0.95
adam_eps = 1e-08
decay_rate = 0.1
step_count = 40

TOK = 256
NB = 32
GROUP = [(dq, dc) for dq in range(4) for dc in range(2) if (dq, dc) != (0, 0)]


def adam_step(weight, moment_one, moment_two, gradient):
    moment_new = beta_one * moment_one + (1.0 - beta_one) * gradient
    second_new = beta_two * moment_two + (1.0 - beta_two) * gradient * gradient
    first_fix = 1.0 - beta_one**step_count
    second_fix = 1.0 - beta_two**step_count
    update = moment_new / first_fix / (jnp.sqrt(second_new / second_fix) + adam_eps)
    weight_new = weight - learn_rate * (update + decay_rate * weight)
    return (weight_new, moment_new, second_new)


def portion_scratch():
    return dict(
        part=pltpu.VMEM((8, NB, 16, 128), BF),
        core_in=pltpu.VMEM((4, NB, 16, 128), BF),
        q1_out=pltpu.VMEM((3, NB, 16, 128), BF),
        q1_in=pltpu.VMEM((3, NB, 16, 128), BF),
        q2_sum=pltpu.VMEM((NB, 16, 128), F32),
        q2_out=pltpu.VMEM((NB, 16, 128), BF),
        q2_in=pltpu.VMEM((3, 8, 16, 128), BF),
        full=pltpu.VMEM((NB, 16, 128), BF),
        pick=pltpu.VMEM((7, 16, 128), BF),
        mine=pltpu.VMEM((8, 16, 128), BF),
    )


def scratch_plan():
    plan = dict(
        state_out=pltpu.VMEM((8, 32, 128), BF),
        state=pltpu.VMEM((8, 8, 32, 128), BF),
        wall=pltpu.VMEM((8, 8, 8, 16, 128), BF),
        mv_pick=pltpu.VMEM((7, 2, 32, 128), BF),
        mv_in=pltpu.VMEM((8, 2, 32, 128), BF),
        wnat=pltpu.VMEM((4096, 256), BF),
        probs=pltpu.VMEM((16, 512, 256), BF),
        keys2=pltpu.VMEM((4, 512, 128), BF),
        vals2=pltpu.VMEM((4, 512, 128), BF),
        bias=pltpu.VMEM((256, 256), F32),
        dacc=pltpu.VMEM((2, 2, 256, 128), F32),
        lacc=pltpu.VMEM((8, 256), F32),
        vacc=pltpu.VMEM((256, 256), F32),
        z_sum=pltpu.VMEM((2, 8, 16, 128), F32),
        z_out=pltpu.VMEM((2, 8, 16, 128), BF),
        z_in=pltpu.VMEM((15, 2, 16, 128), BF),
        z_all=pltpu.VMEM((2, 8, 16, 128), BF),
        tok=pltpu.VMEM((TOK, 4096), BF),
        q=pltpu.VMEM((TOK, 2048), BF),
        k=pltpu.VMEM((TOK, 256), BF),
        cot=pltpu.VMEM((TOK, 2048), BF),
        doc=pltpu.VMEM((1, TOK), jnp.int32),
        w=pltpu.VMEM((64, 256), F32),
        m=pltpu.VMEM((64, 256), F32),
        v=pltpu.VMEM((64, 256), F32),
    )
    for name in "ab":
        for key, value in portion_scratch().items():
            plan[name + "_" + key] = value
    plan["send"] = pltpu.SemaphoreType.DMA((112,))
    plan["recv"] = pltpu.SemaphoreType.DMA((112,))
    plan["local"] = pltpu.SemaphoreType.DMA((8,))
    return plan


PLAN = scratch_plan()


def doubled(pair, odd):
    lane = lax.broadcasted_iota(jnp.int32, pair.shape, 1)
    turned = pltpu.roll(pair, 64, 1)
    low, high = (turned, pair) if odd else (pair, turned)
    top = jnp.where(lane < 64, low, 0.0)
    bottom = jnp.where(lane >= 64, high, 0.0)
    return jnp.concatenate([top, bottom], axis=0)


def kernel(
    table_ref, trig_ref, w_hbm, m_hbm, v_hbm, k_hbm, doc_hbm, q_hbm, cot_hbm, tok_hbm,
    wo_ref, mo_ref, vo_ref, loss_ref, *scratch
):
    s = dict(zip(PLAN, scratch))
    send, recv = s["send"], s["recv"]
    w_ref, m_ref, v_ref, k_ref, doc_ref, q_ref, cot_ref, tok_ref = (
        s[name] for name in ("w", "m", "v", "k", "doc", "q", "cot", "tok")
    )
    fetches = {}
    for idx, (name, src) in enumerate(
        zip(("w", "m", "v", "k", "doc", "q", "cot", "tok"), (w_hbm, m_hbm, v_hbm, k_hbm, doc_hbm, q_hbm, cot_hbm, tok_hbm))
    ):
        fetches[name] = pltpu.make_async_copy(src, s[name], s["local"].at[idx])
        fetches[name].start()
    rep = lax.axis_index("rep")
    fs = lax.axis_index("fsdp")
    y = lax.div(rep, 2)
    x = lax.div(fs, 16)
    zl = lax.rem(lax.div(fs, 2), 8)
    core = lax.rem(fs, 2)
    z = lax.rem(rep, 2) * 8 + zl
    xs = [x] + [lax.rem(x + d, 4) for d in (1, 2, 3)]
    ys = [y] + [lax.rem(y + d, 4) for d in (1, 2, 3)]
    cores = [core, 1 - core]
    me_c = x * 2 + core

    def dev(dx=0, dy=0, dz=0, dc=0):
        if dz == 0:
            return (ys[dy] * 2 + lax.rem(rep, 2), xs[dx] * 16 + zl * 2 + cores[dc])
        nz = lax.rem(z + (dz + 16), 16)
        return (ys[dy] * 2 + lax.div(nz, 8), xs[dx] * 16 + lax.rem(nz, 8) * 2 + cores[dc])

    def new_of(dx, dc):
        return table_ref[64 + xs[dx] * 16 + zl * 2 + cores[dc]]

    used = [0]
    pending = []

    def copy(src, dst, where):
        idx = used[0]
        used[0] += 1
        made = pltpu.make_async_remote_copy(
            src_ref=src, dst_ref=dst, send_sem=send.at[idx], recv_sem=recv.at[idx],
            device_id=where, device_id_type=MESH,
        )
        made.start()
        pending.append(made)
        return made

    def arrive(copies):
        for made in copies:
            made.wait_recv()

    barrier = pltpu.get_barrier_semaphore()
    partners = [dict(dx=dq, dc=dc) for dq, dc in GROUP]
    partners += [dict(dy=dq, dc=dc) for dq, dc in GROUP if dq]
    partners += [dict(dz=dz) for dz in range(1, 16)]
    for partner in partners:
        pl.semaphore_signal(barrier, inc=1, device_id=dev(**partner), device_id_type=MESH)

    lane128 = lax.broadcasted_iota(jnp.int32, (TOK, 128), 1)
    low_half = (lane128 % 64) < 32

    def rotated(pair):
        swapped = jnp.where(low_half, pltpu.roll(pair, 96, 1), pltpu.roll(pair, 32, 1))
        return pair * trig_ref[:, 0:128] + swapped * trig_ref[:, 128:256]

    for name in ("w", "m", "v"):
        fetches[name].wait()
    for c in range(8):
        rows, cols = pl.ds(16 * (c // 2), 16), pl.ds(128 * (c % 2), 128)
        s["wall"][me_c, 3, c] = w_ref[rows, cols].astype(BF)
        for part, ref in enumerate((m_ref, v_ref)):
            s["state_out"][c, 16 * part:16 * part + 16] = ref[rows, cols].astype(BF)
    s["state"][3, me_c] = s["state_out"][me_c]

    fetches["k"].wait()
    for i in range(2):
        turned = rotated(k_ref[:, 128 * i:128 * i + 128].astype(F32))
        for odd in range(2):
            s["keys2"][2 * i + odd] = doubled(turned, odd).astype(BF)
    fetches["doc"].wait()
    docs = doc_ref[...].astype(F32)
    columns = jnp.transpose(jnp.broadcast_to(docs, (128, TOK)))
    own_row = lax.broadcasted_iota(jnp.int32, (TOK, 128), 0)
    for half in range(2):
        allowed = (own_row <= lane128 + 128 * half) & (columns == docs[:, 128 * half:128 * half + 128])
        s["bias"][:, 128 * half:128 * half + 128] = jnp.where(allowed, 0.0, -1e30)

    pl.semaphore_wait(barrier, len(partners))
    wall = s["wall"]
    own_w = wall.at[me_c, 3]
    along_z = [copy(own_w, wall.at[me_c, 3 - o], dev(dz=o)) for o in (-4, 3, -3, 2, -2, 1, -1)]
    first = []
    for dq, dc in GROUP:
        to_c = xs[dq] * 2 + cores[dc]
        first.append(copy(s["state_out"].at[to_c], s["state"].at[3, me_c], dev(dx=dq, dc=dc)))
    fetches["q"].wait()
    fetches["cot"].wait()
    factor = 0.125 * math.log2(math.e)

    def softmax(keys, queries, bias):
        scores = lax.dot_general(keys, queries, (((1,), (1,)), ((), ())), preferred_element_type=F32)
        scores = scores * factor + bias
        raised = jnp.exp2(scores - jnp.max(scores, axis=0, keepdims=True))
        return (raised * (1.0 / jnp.sum(raised, axis=0, keepdims=True))).astype(BF)

    def attention(g):
        def pair_step(i, _):
            q = 4 * g + i
            cols = pl.ds(pl.multiple_of(q * 128, 128), 128)
            rq = rotated(q_ref[:, cols].astype(F32)).astype(BF)
            cot = cot_ref[:, cols]
            for odd in range(2):
                early = softmax(s["keys2"][g, 256 * odd:256 * odd + 128, :], rq[0:128], s["bias"][0:128, 0:128])
                late = softmax(s["keys2"][g, 256 * odd:256 * odd + 256, :], rq[128:256], s["bias"][:, 128:256])
                early = jnp.concatenate([early, jnp.zeros((128, 128), BF)], axis=0)
                probs = jnp.concatenate([early, late], axis=1)
                s["probs"][q, 256 * odd:256 * odd + 256, :] = probs
                s["dacc"][g % 2, odd] += jnp.dot(probs, cot, preferred_element_type=F32)
            return 0

        s["dacc"][g % 2] = jnp.zeros((2, 256, 128), F32)
        lax.fori_loop(0, 4, pair_step, 0, unroll=2)

    def partial(name):
        d = s["dacc"]
        low = d[0, 0] + pltpu.roll(d[0, 1], 64, 1)
        high = pltpu.roll(d[1, 0], 64, 1) + d[1, 1]
        grad = jnp.where(lane128 < 64, low, high)
        turned = jnp.transpose(grad).astype(BF)
        out = s[name + "_part"]

        def block(i, _):
            r = jnp.dot(turned, tok_ref[:, pl.ds(pl.multiple_of(i * 512, 512), 512)], preferred_element_type=F32)
            r = r.astype(BF)
            for k in range(4):
                for p in range(8):
                    out[p, 4 * i + k] = r[16 * p:16 * p + 16, 128 * k:128 * k + 128]
            return 0

        lax.fori_loop(0, 8, block, 0)

    def f(value):
        return value.astype(F32)

    def over(n, step, body):
        def run(i, _):
            body(pl.ds(i * step, step))
            return 0

        lax.fori_loop(0, n // step, run, 0)

    class Portion:
        def __init__(self, name):
            self.name = name
            self.q1, self.q2 = (x, y) if name == "a" else (y, x)
            self.q1s, self.q2s = (xs, ys) if name == "a" else (ys, xs)
            self.side = 0 if name == "a" else 1

        def buf(self, key):
            return s[self.name + "_" + key]

        def at1(self, r, dc=0):
            return dev(dx=r, dc=dc) if self.name == "a" else dev(dy=r, dc=dc)

        def at2(self, r):
            return dev(dy=r) if self.name == "a" else dev(dx=r)

        def send_core(self):
            self.c0 = [copy(self.buf("part").at[pl.ds(4 * (1 - core), 4)], self.buf("core_in"), dev(dc=1))]

        def send_q1(self):
            arrive(self.c0)
            part, came, out = self.buf("part"), self.buf("core_in"), self.buf("q1_out")
            self.c1 = []
            for r in (2, 1, 3):
                to = self.q1s[r]

                def add(n):
                    out[r - 1, n] = (f(part[core * 4 + to, n]) + f(came[to, n])).astype(BF)

                over(NB, 4, add)
                self.c1.append(copy(out.at[r - 1], self.buf("q1_in").at[r - 1], self.at1(r)))

        def send_q2(self):
            arrive(self.c1)
            part, came, got = self.buf("part"), self.buf("core_in"), self.buf("q1_in")
            total, out = self.buf("q2_sum"), self.buf("q2_out")

            def add(n):
                t = f(part[core * 4 + self.q1, n]) + f(came[self.q1, n])
                t = t + f(got[0, n]) + f(got[1, n]) + f(got[2, n])
                total[n] = t
                out[n] = t.astype(BF)

            over(NB, 4, add)
            self.c2 = []
            for r in (2, 1, 3):
                to = self.q2s[r]
                self.c2.append(copy(out.at[pl.ds(8 * to, 8)], self.buf("q2_in").at[r - 1], self.at2(r)))

        def sum_q2(self):
            arrive(self.c2)
            got, side = self.buf("q2_in"), self.side
            t = self.buf("q2_sum")[pl.ds(8 * self.q2, 8)]
            t = t + f(got[0]) + f(got[1]) + f(got[2])
            s["z_sum"][side] = t
            s["z_out"][side] = t.astype(BF)

        def gather_q2(self):
            full, mine = self.buf("full"), s["z_all"].at[self.side]
            own = pl.ds(8 * self.q2, 8)
            self.c6 = [copy(mine, full.at[own], self.at2(r)) for r in (2, 1, 3)]
            full[own] = mine[...]

        def exchange(self):
            arrive(self.c6)
            full, pick, mine = self.buf("full"), self.buf("pick"), self.buf("mine")
            piece = core * 4 + self.q1
            self.c7 = []
            for idx, (dq, dc) in enumerate(GROUP):
                pick[idx] = full[new_of(dq if self.name == "a" else 0, dc)]
                self.c7.append(copy(pick.at[idx], mine.at[piece], self.at1(dq, dc)))
            mine[piece] = full[new_of(0, 0)]

        def gradient(self):
            arrive(self.c7)
            return jnp.transpose(f(self.buf("mine")[...]).reshape(128, 128))

    pa, pb = Portion("a"), Portion("b")
    state = s["state"]

    def z_step(step):
        up, down = 3 + (step - 1), 3 - (step - 1)
        if step < 4:
            pairs = [(up, up + 1, 15, pl.ds(0, 8)), (down, down - 1, 1, pl.ds(0, 8))]
        else:
            pairs = [(6, 7, 15, pl.ds(0, 4)), (0, 7, 1, pl.ds(4, 4))]
        return [copy(state.at[src, part], state.at[dst, part], dev(dz=dz)) for src, dst, dz, part in pairs]

    def where(j):
        return lax.rem(lax.rem(lax.div(j, 2), 8) - zl + 11, 8), lax.div(j, 16) * 2 + lax.rem(j, 2)

    def wcopy(c, part, where_to):
        return copy(wall.at[c, part], wall.at[c, part], where_to)

    all_z = pl.ds(0, 8)
    left_c, right_c = xs[3] * 2 + core, xs[1] * 2 + core
    far_c = xs[2] * 2 + core
    own_n = new_of(0, 0)

    attention(0)
    attention(1)
    fetches["tok"].wait()
    partial("a")
    pa.send_core()
    attention(2)
    pa.send_q1()
    attention(3)
    partial("b")
    pb.send_core()
    arrive(along_z)
    arrive(first)
    ring = z_step(1)
    pb.send_q1()
    along_x = [wcopy(me_c, all_z, dev(dx=1)), wcopy(me_c, all_z, dev(dx=3))]
    across = [wcopy(me_c, all_z, dev(dc=1))]
    arrive(ring)
    ring = z_step(2)
    pa.send_q2()
    arrive(ring)
    ring = z_step(3)
    pb.send_q2()
    pa.sum_q2()
    pb.sum_q2()

    z_out, z_in, z_all = s["z_out"], s["z_in"], s["z_all"]
    z_copies = []
    for r in sorted(range(1, 16), key=lambda r: -min(r, 16 - r)):
        z_copies.append(copy(z_out.at[:, lax.rem(zl + r, 8)], z_in.at[r - 1], dev(dz=r)))
    arrive(along_x)
    far = [wcopy(left_c, pl.ds(0, 4), dev(dx=1)), wcopy(right_c, pl.ds(4, 4), dev(dx=3))]
    across += [wcopy(left_c, all_z, dev(dc=1)), wcopy(right_c, all_z, dev(dc=1))]
    arrive(ring)
    ring = z_step(4)
    s["vacc"][...] = jnp.zeros((256, 256), F32)
    s["lacc"][...] = jnp.zeros((8, 256), F32)
    arrive(z_copies)
    t = s["z_sum"][:, zl]
    for r in range(15):
        t = t + f(z_in[r])
    z_all[:, zl] = t.astype(BF)
    gathered = [copy(z_all.at[:, zl], z_all.at[:, zl], dev(dz=o)) for o in (4, 13, 3, 14, 2, 15, 1)]

    arrive(ring)
    moved = []
    for idx, (dq, dc) in enumerate(GROUP):
        n = new_of(dq, dc)
        for i in range(2):
            slot, c = where(table_ref[2 * n + i])
            s["mv_pick"][idx, i] = state[slot, c]
        moved.append(copy(s["mv_pick"].at[idx], s["mv_in"].at[me_c], dev(dx=dq, dc=dc)))
    for i in range(2):
        slot, c = where(table_ref[2 * own_n + i])
        s["mv_in"][me_c, i] = state[slot, c]
    arrive(far)
    across.append(wcopy(far_c, all_z, dev(dc=1)))
    arrive(gathered)
    pa.gather_q2()
    pb.gather_q2()

    wnat = s["wnat"]
    arrive(across)

    def natural(i, _):
        slot, c = where(table_ref[i])
        base = pl.multiple_of(i * 64, 64)
        for piece in range(8):
            wnat[pl.ds(base + 16 * (piece // 2), 16), 128 * (piece % 2):128 * (piece % 2) + 128] = wall[c, slot, piece]
        return 0

    lax.fori_loop(0, 64, natural, 0, unroll=2)

    def project(i, _):
        k = pl.ds(pl.multiple_of(i * 512, 512), 512)
        s["vacc"][...] += jnp.dot(tok_ref[:, k], wnat[k, :], preferred_element_type=F32)
        return 0

    lax.fori_loop(0, 8, project, 0)
    for i in range(2):
        pair = s["vacc"][:, 128 * i:128 * i + 128]
        for odd in range(2):
            s["vals2"][2 * i + odd] = doubled(pair, odd).astype(BF)

    def loss_step(q, _):
        cot = cot_ref[:, pl.ds(pl.multiple_of(q * 128, 128), 128)]
        t = lax.dot_general(s["vals2"][lax.div(q, 4)], cot, (((1,), (1,)), ((), ())), preferred_element_type=F32)
        t = t * f(s["probs"][q])
        s["lacc"][...] += jnp.sum(t.reshape(64, 8, 256), axis=0)
        return 0

    pa.exchange()
    pb.exchange()
    lax.fori_loop(0, 16, loss_step, 0)
    loss_ref[...] = jnp.sum(s["lacc"][...], axis=0, keepdims=True)

    arrive(moved)
    for made in pending[:-14]:
        made.wait_send()
    grads = [pa.gradient(), pb.gradient()]
    for i in range(2):
        slot, src = where(table_ref[2 * own_n + i])
        for c in range(8):
            r0, l0 = 64 * i + 16 * (c // 2), 128 * (c % 2)
            weight = f(wall[src, slot, c])
            one = f(s["mv_in"][c, i, 0:16])
            two = f(s["mv_in"][c, i, 16:32])
            new = adam_step(weight, one, two, grads[c % 2][r0:r0 + 16])
            for ref, value in zip((wo_ref, mo_ref, vo_ref), new):
                ref[r0:r0 + 16, l0:l0 + 128] = value
    for made in pending[-14:]:
        made.wait_send()


def shards(
    tokens, queries, key_vectors, cotangent, positions, doc_ids, weight, moment_one, moment_two, old_ids, new_ids
):
    index = jnp.arange(64, dtype=jnp.int32)
    entry = jnp.arange(128, dtype=jnp.int32)
    table = jnp.sum(
        jnp.where(old_ids[None, :] == entry[:, None], index[None, :], 0)
        + jnp.where(index[None, :] + 64 == entry[:, None], new_ids[None, :], 0),
        axis=1,
    )
    lane = jnp.arange(256, dtype=jnp.int32)
    half = (lane % 32).astype(F32)
    frequency = rope_base ** (-(half * 2.0 / 64))
    angles = positions.astype(F32)[:, None] * frequency[None, :]
    signed = jnp.where((lane % 64) < 32, -jnp.sin(angles), jnp.sin(angles))
    trig = jnp.where(lane < 128, jnp.cos(angles), signed)

    vmem = pl.BlockSpec(memory_space=pltpu.VMEM)
    smem = pl.BlockSpec(memory_space=pltpu.SMEM)
    outs = pl.pallas_call(
        kernel,
        out_shape=[jax.ShapeDtypeStruct((128, 256), F32)] * 3 + [jax.ShapeDtypeStruct((1, 256), F32)],
        in_specs=[smem, vmem] + [pl.BlockSpec(memory_space=pl.ANY)] * 8,
        out_specs=[vmem] * 4,
        scratch_shapes=list(PLAN.values()),
        compiler_params=pltpu.CompilerParams(
            collective_id=0, has_side_effects=True, vmem_limit_bytes=54144 * 1024
        ),
        cost_estimate=pl.CostEstimate(flops=2_200_000_000, bytes_accessed=6_000_000, transcendentals=2_200_000),
    )(
        table, trig, weight, moment_one, moment_two, key_vectors, doc_ids.reshape(1, 256), queries, cotangent, tokens
    )
    return (outs[0], outs[1], outs[2], outs[3].reshape(256))


def solution(mesh):
    in_specs = (
        P(("rep", "fsdp"), None),
        P(("rep", "fsdp"), None),
        P(("rep", "fsdp"), None),
        P(("rep", "fsdp"), None),
        P(("rep", "fsdp")),
        P(("rep", "fsdp")),
        P("fsdp", None),
        P("fsdp", None),
        P("fsdp", None),
        P(),
        P(),
    )
    out_specs = (P("fsdp", None), P("fsdp", None), P("fsdp", None), P(("rep", "fsdp")))
    return jax.shard_map(shards, mesh=mesh, in_specs=in_specs, out_specs=out_specs, check_vma=False)
```

```python
import math

import jax
import jax.numpy as jnp
from jax import lax
from jax.experimental import pallas as pl
from jax.experimental.pallas import tpu as pltpu
from jax.sharding import PartitionSpec as P

MESH = pl.DeviceIdType.MESH
BF = jnp.bfloat16
F32 = jnp.float32

rope_base = 500000.0
learn_rate = 0.0003 * math.sqrt(2.0)
beta_one = 0.9
beta_two = 0.95
adam_eps = 1e-08
decay_rate = 0.1
step_count = 40

TOK = 256
NB = 32
GROUP = [(dq, dc) for dq in range(4) for dc in range(2) if (dq, dc) != (0, 0)]


def adam_step(weight, moment_one, moment_two, gradient):
    moment_new = beta_one * moment_one + (1.0 - beta_one) * gradient
    second_new = beta_two * moment_two + (1.0 - beta_two) * gradient * gradient
    first_fix = 1.0 - beta_one**step_count
    second_fix = 1.0 - beta_two**step_count
    update = moment_new / first_fix / (jnp.sqrt(second_new / second_fix) + adam_eps)
    weight_new = weight - learn_rate * (update + decay_rate * weight)
    return (weight_new, moment_new, second_new)


def portion_scratch():
    return dict(
        part=pltpu.VMEM((8, NB, 16, 128), BF),
        core_in=pltpu.VMEM((4, NB, 16, 128), BF),
        q1_out=pltpu.VMEM((3, NB, 16, 128), BF),
        q1_in=pltpu.VMEM((3, NB, 16, 128), BF),
        q2_sum=pltpu.VMEM((NB, 16, 128), F32),
        q2_out=pltpu.VMEM((NB, 16, 128), BF),
        q2_in=pltpu.VMEM((3, 8, 16, 128), BF),
        full=pltpu.VMEM((NB, 16, 128), BF),
        pick=pltpu.VMEM((7, 16, 128), BF),
        mine=pltpu.VMEM((8, 16, 128), BF),
    )


def scratch_plan():
    plan = dict(
        state_out=pltpu.VMEM((8, 32, 128), BF),
        state=pltpu.VMEM((8, 8, 32, 128), BF),
        wall=pltpu.VMEM((8, 8, 8, 16, 128), BF),
        mv_pick=pltpu.VMEM((7, 2, 32, 128), BF),
        mv_in=pltpu.VMEM((8, 2, 32, 128), BF),
        wnat=pltpu.VMEM((4096, 256), BF),
        probs=pltpu.VMEM((16, 512, 256), BF),
        keys2=pltpu.VMEM((4, 512, 128), BF),
        vals2=pltpu.VMEM((4, 512, 128), BF),
        bias=pltpu.VMEM((256, 256), F32),
        dacc=pltpu.VMEM((2, 2, 256, 128), F32),
        lacc=pltpu.VMEM((8, 256), F32),
        vacc=pltpu.VMEM((256, 256), F32),
        z_sum=pltpu.VMEM((2, 8, 16, 128), F32),
        z_out=pltpu.VMEM((2, 8, 16, 128), BF),
        z_in=pltpu.VMEM((15, 2, 16, 128), BF),
        z_all=pltpu.VMEM((2, 8, 16, 128), BF),
        tok=pltpu.VMEM((TOK, 4096), BF),
        q=pltpu.VMEM((TOK, 2048), BF),
        cot=pltpu.VMEM((TOK, 2048), BF),
    )
    for name in "ab":
        for key, value in portion_scratch().items():
            plan[name + "_" + key] = value
    plan["send"] = pltpu.SemaphoreType.DMA((112,))
    plan["recv"] = pltpu.SemaphoreType.DMA((112,))
    plan["local"] = pltpu.SemaphoreType.DMA((3,))
    return plan


PLAN = scratch_plan()


def doubled(pair, odd):
    lane = lax.broadcasted_iota(jnp.int32, pair.shape, 1)
    turned = pltpu.roll(pair, 64, 1)
    low, high = (turned, pair) if odd else (pair, turned)
    top = jnp.where(lane < 64, low, 0.0)
    bottom = jnp.where(lane >= 64, high, 0.0)
    return jnp.concatenate([top, bottom], axis=0)


def kernel(
    table_ref, trig_ref, small_ref, k_ref, doc_ref, q_hbm, cot_hbm, tok_hbm,
    wo_ref, mo_ref, vo_ref, go_ref, loss_ref, *scratch
):
    s = dict(zip(PLAN, scratch))
    send, recv = s["send"], s["recv"]
    q_ref, cot_ref, tok_ref = s["q"], s["cot"], s["tok"]
    fetches = {}
    for idx, (name, src) in enumerate(zip(("q", "cot", "tok"), (q_hbm, cot_hbm, tok_hbm))):
        fetches[name] = pltpu.make_async_copy(src, s[name], s["local"].at[idx])
        fetches[name].start()
    rep = lax.axis_index("rep")
    fs = lax.axis_index("fsdp")
    y = lax.div(rep, 2)
    x = lax.div(fs, 16)
    zl = lax.rem(lax.div(fs, 2), 8)
    core = lax.rem(fs, 2)
    z = lax.rem(rep, 2) * 8 + zl
    xs = [x] + [lax.rem(x + d, 4) for d in (1, 2, 3)]
    ys = [y] + [lax.rem(y + d, 4) for d in (1, 2, 3)]
    cores = [core, 1 - core]
    me_c = x * 2 + core

    def dev(dx=0, dy=0, dz=0, dc=0):
        if dz == 0:
            return (ys[dy] * 2 + lax.rem(rep, 2), xs[dx] * 16 + zl * 2 + cores[dc])
        nz = lax.rem(z + (dz + 16), 16)
        return (ys[dy] * 2 + lax.div(nz, 8), xs[dx] * 16 + lax.rem(nz, 8) * 2 + cores[dc])

    def new_of(dx, dc):
        return table_ref[64 + xs[dx] * 16 + zl * 2 + cores[dc]]

    used = [0]
    pending = []

    def copy(src, dst, where):
        idx = used[0]
        used[0] += 1
        made = pltpu.make_async_remote_copy(
            src_ref=src, dst_ref=dst, send_sem=send.at[idx], recv_sem=recv.at[idx],
            device_id=where, device_id_type=MESH,
        )
        made.start()
        pending.append(made)
        return made

    def arrive(copies):
        for made in copies:
            made.wait_recv()

    barrier = pltpu.get_barrier_semaphore()
    partners = [dict(dx=dq, dc=dc) for dq, dc in GROUP]
    partners += [dict(dy=dq, dc=dc) for dq, dc in GROUP if dq]
    partners += [dict(dz=dz) for dz in range(1, 16)]
    for partner in partners:
        pl.semaphore_signal(barrier, inc=1, device_id=dev(**partner), device_id_type=MESH)

    lane128 = lax.broadcasted_iota(jnp.int32, (TOK, 128), 1)
    low_half = (lane128 % 64) < 32

    def rotated(pair):
        swapped = jnp.where(low_half, pltpu.roll(pair, 96, 1), pltpu.roll(pair, 32, 1))
        return pair * trig_ref[:, 0:128] + swapped * trig_ref[:, 128:256]

    for c in range(8):
        r0, l0 = 16 * (c // 2), 128 * (c % 2)
        s["wall"][me_c, 3, c] = small_ref[r0:r0 + 16, l0:l0 + 128].astype(BF)
        for part in range(2):
            moment = small_ref[64 + 64 * part + r0:80 + 64 * part + r0, l0:l0 + 128]
            s["state_out"][c, 16 * part:16 * part + 16] = moment.astype(BF)
    s["state"][3, me_c] = s["state_out"][me_c]

    for i in range(2):
        turned = rotated(k_ref[:, 128 * i:128 * i + 128].astype(F32))
        for odd in range(2):
            s["keys2"][2 * i + odd] = doubled(turned, odd).astype(BF)
    docs = doc_ref[...].astype(F32)
    columns = jnp.transpose(jnp.broadcast_to(docs, (128, TOK)))
    own_row = lax.broadcasted_iota(jnp.int32, (TOK, 128), 0)
    for half in range(2):
        allowed = (own_row <= lane128 + 128 * half) & (columns == docs[:, 128 * half:128 * half + 128])
        s["bias"][:, 128 * half:128 * half + 128] = jnp.where(allowed, 0.0, -1e30)

    fetches["q"].wait()
    fetches["cot"].wait()
    factor = 0.125 * math.log2(math.e)

    def softmax(keys, queries, bias):
        scores = lax.dot_general(keys, queries, (((1,), (1,)), ((), ())), preferred_element_type=F32)
        scores = scores * factor + bias
        raised = jnp.exp2(scores - jnp.max(scores, axis=0, keepdims=True))
        return (raised * (1.0 / jnp.sum(raised, axis=0, keepdims=True))).astype(BF)

    def attention(g):
        def pair_step(i, _):
            q = 4 * g + i
            cols = pl.ds(pl.multiple_of(q * 128, 128), 128)
            rq = rotated(q_ref[:, cols].astype(F32)).astype(BF)
            cot = cot_ref[:, cols]
            for odd in range(2):
                early = softmax(s["keys2"][g, 256 * odd:256 * odd + 128, :], rq[0:128], s["bias"][0:128, 0:128])
                late = softmax(s["keys2"][g, 256 * odd:256 * odd + 256, :], rq[128:256], s["bias"][:, 128:256])
                early = jnp.concatenate([early, jnp.zeros((128, 128), BF)], axis=0)
                probs = jnp.concatenate([early, late], axis=1)
                s["probs"][q, 256 * odd:256 * odd + 256, :] = probs
                s["dacc"][g % 2, odd] += jnp.dot(probs, cot, preferred_element_type=F32)
            return 0

        s["dacc"][g % 2] = jnp.zeros((2, 256, 128), F32)
        lax.fori_loop(0, 4, pair_step, 0, unroll=2)

    def partial(name):
        d = s["dacc"]
        low = d[0, 0] + pltpu.roll(d[0, 1], 64, 1)
        high = pltpu.roll(d[1, 0], 64, 1) + d[1, 1]
        grad = jnp.where(lane128 < 64, low, high)
        turned = jnp.transpose(grad).astype(BF)
        out = s[name + "_part"]

        def block(i, _):
            r = jnp.dot(turned, tok_ref[:, pl.ds(pl.multiple_of(i * 512, 512), 512)], preferred_element_type=F32)
            r = r.astype(BF)
            for k in range(4):
                for p in range(8):
                    out[p, 4 * i + k] = r[16 * p:16 * p + 16, 128 * k:128 * k + 128]
            return 0

        lax.fori_loop(0, 8, block, 0)

    def f(value):
        return value.astype(F32)

    def over(n, step, body):
        def run(i, _):
            body(pl.ds(i * step, step))
            return 0

        lax.fori_loop(0, n // step, run, 0, unroll=2)

    class Portion:
        def __init__(self, name):
            self.name = name
            self.q1, self.q2 = (x, y) if name == "a" else (y, x)
            self.q1s, self.q2s = (xs, ys) if name == "a" else (ys, xs)
            self.side = 0 if name == "a" else 1

        def buf(self, key):
            return s[self.name + "_" + key]

        def at1(self, r, dc=0):
            return dev(dx=r, dc=dc) if self.name == "a" else dev(dy=r, dc=dc)

        def at2(self, r):
            return dev(dy=r) if self.name == "a" else dev(dx=r)

        def send_core(self):
            self.c0 = [copy(self.buf("part").at[pl.ds(4 * (1 - core), 4)], self.buf("core_in"), dev(dc=1))]

        def send_q1(self):
            arrive(self.c0)
            part, came, out = self.buf("part"), self.buf("core_in"), self.buf("q1_out")
            self.c1 = []
            for r in (2, 1, 3):
                to = self.q1s[r]

                def add(n):
                    out[r - 1, n] = (f(part[core * 4 + to, n]) + f(came[to, n])).astype(BF)

                over(NB, 4, add)
                self.c1.append(copy(out.at[r - 1], self.buf("q1_in").at[r - 1], self.at1(r)))

        def send_q2(self):
            arrive(self.c1)
            part, came, got = self.buf("part"), self.buf("core_in"), self.buf("q1_in")
            total, out = self.buf("q2_sum"), self.buf("q2_out")

            def add(n):
                t = f(part[core * 4 + self.q1, n]) + f(came[self.q1, n])
                t = t + f(got[0, n]) + f(got[1, n]) + f(got[2, n])
                total[n] = t
                out[n] = t.astype(BF)

            over(NB, 4, add)
            self.c2 = []
            for r in (2, 1, 3):
                to = self.q2s[r]
                self.c2.append(copy(out.at[pl.ds(8 * to, 8)], self.buf("q2_in").at[r - 1], self.at2(r)))

        def sum_q2(self):
            arrive(self.c2)
            got, side = self.buf("q2_in"), self.side
            t = self.buf("q2_sum")[pl.ds(8 * self.q2, 8)]
            t = t + f(got[0]) + f(got[1]) + f(got[2])
            s["z_sum"][side] = t
            s["z_out"][side] = t.astype(BF)

        def gather_q2(self):
            full, mine = self.buf("full"), s["z_all"].at[self.side]
            own = pl.ds(8 * self.q2, 8)
            self.c6 = [copy(mine, full.at[own], self.at2(r)) for r in (2, 1, 3)]
            full[own] = mine[...]

        def exchange(self):
            arrive(self.c6)
            full, pick, mine = self.buf("full"), self.buf("pick"), self.buf("mine")
            piece = core * 4 + self.q1
            self.c7 = []
            for idx, (dq, dc) in enumerate(GROUP):
                pick[idx] = full[new_of(dq if self.name == "a" else 0, dc)]
                self.c7.append(copy(pick.at[idx], mine.at[piece], self.at1(dq, dc)))
            mine[piece] = full[new_of(0, 0)]

        def gradient(self):
            arrive(self.c7)
            return jnp.transpose(f(self.buf("mine")[...]).reshape(128, 128))

    pa, pb = Portion("a"), Portion("b")
    state = s["state"]

    def z_step(step):
        up, down = 3 + (step - 1), 3 - (step - 1)
        if step < 4:
            pairs = [(up, up + 1, 15, pl.ds(0, 8)), (down, down - 1, 1, pl.ds(0, 8))]
        else:
            pairs = [(6, 7, 15, pl.ds(0, 4)), (0, 7, 1, pl.ds(4, 4))]
        return [copy(state.at[src, part], state.at[dst, part], dev(dz=dz)) for src, dst, dz, part in pairs]

    def where(j):
        return lax.rem(lax.rem(lax.div(j, 2), 8) - zl + 11, 8), lax.div(j, 16) * 2 + lax.rem(j, 2)

    def wcopy(c, part, where_to):
        return copy(wall.at[c, part], wall.at[c, part], where_to)

    all_z = pl.ds(0, 8)
    left_c, right_c = xs[3] * 2 + core, xs[1] * 2 + core
    far_c = xs[2] * 2 + core
    own_n = new_of(0, 0)

    attention(0)
    attention(1)
    pl.semaphore_wait(barrier, len(partners))
    wall = s["wall"]
    own_w = wall.at[me_c, 3]
    along_z = [copy(own_w, wall.at[me_c, 3 - o], dev(dz=o)) for o in (-4, 3, -3, 2, -2, 1, -1)]
    first = []
    for dq, dc in GROUP:
        to_c = xs[dq] * 2 + cores[dc]
        first.append(copy(s["state_out"].at[to_c], s["state"].at[3, me_c], dev(dx=dq, dc=dc)))
    fetches["tok"].wait()
    partial("a")
    pa.send_core()
    attention(2)
    pa.send_q1()
    attention(3)
    partial("b")
    pb.send_core()
    arrive(along_z)
    arrive(first)
    ring = z_step(1)
    pb.send_q1()
    along_x = [wcopy(me_c, all_z, dev(dx=1)), wcopy(me_c, all_z, dev(dx=3))]
    across = [wcopy(me_c, all_z, dev(dc=1))]
    arrive(ring)
    ring = z_step(2)
    pa.send_q2()
    arrive(ring)
    ring = z_step(3)
    pb.send_q2()
    pa.sum_q2()
    pb.sum_q2()

    z_out, z_in, z_all = s["z_out"], s["z_in"], s["z_all"]
    z_copies = []
    for r in sorted(range(1, 16), key=lambda r: -min(r, 16 - r)):
        z_copies.append(copy(z_out.at[:, lax.rem(zl + r, 8)], z_in.at[r - 1], dev(dz=r)))
    arrive(along_x)
    far = [wcopy(left_c, pl.ds(0, 4), dev(dx=1)), wcopy(right_c, pl.ds(4, 4), dev(dx=3))]
    across += [wcopy(left_c, all_z, dev(dc=1)), wcopy(right_c, all_z, dev(dc=1))]
    arrive(ring)
    ring = z_step(4)
    s["vacc"][...] = jnp.zeros((256, 256), F32)
    s["lacc"][...] = jnp.zeros((8, 256), F32)
    arrive(z_copies)
    t = s["z_sum"][:, zl]
    for r in range(15):
        t = t + f(z_in[r])
    z_all[:, zl] = t.astype(BF)
    gathered = [copy(z_all.at[:, zl], z_all.at[:, zl], dev(dz=o)) for o in (4, 13, 3, 14, 2, 15, 1)]

    arrive(ring)
    moved = []
    for idx, (dq, dc) in enumerate(GROUP):
        n = new_of(dq, dc)
        for i in range(2):
            slot, c = where(table_ref[2 * n + i])
            s["mv_pick"][idx, i] = state[slot, c]
        moved.append(copy(s["mv_pick"].at[idx], s["mv_in"].at[me_c], dev(dx=dq, dc=dc)))
    for i in range(2):
        slot, c = where(table_ref[2 * own_n + i])
        s["mv_in"][me_c, i] = state[slot, c]
    arrive(far)
    across.append(wcopy(far_c, all_z, dev(dc=1)))
    arrive(gathered)
    pa.gather_q2()
    pb.gather_q2()

    wnat = s["wnat"]
    arrive(across)

    def natural(i, _):
        slot, c = where(table_ref[i])
        base = pl.multiple_of(i * 64, 64)
        for piece in range(8):
            wnat[pl.ds(base + 16 * (piece // 2), 16), 128 * (piece % 2):128 * (piece % 2) + 128] = wall[c, slot, piece]
        return 0

    lax.fori_loop(0, 64, natural, 0, unroll=2)

    def project(i, _):
        k = pl.ds(pl.multiple_of(i * 512, 512), 512)
        s["vacc"][...] += jnp.dot(tok_ref[:, k], wnat[k, :], preferred_element_type=F32)
        return 0

    lax.fori_loop(0, 8, project, 0)
    for i in range(2):
        pair = s["vacc"][:, 128 * i:128 * i + 128]
        for odd in range(2):
            s["vals2"][2 * i + odd] = doubled(pair, odd).astype(BF)

    def loss_step(q, _):
        cot = cot_ref[:, pl.ds(pl.multiple_of(q * 128, 128), 128)]
        t = lax.dot_general(s["vals2"][lax.div(q, 4)], cot, (((1,), (1,)), ((), ())), preferred_element_type=F32)
        t = t * f(s["probs"][q])
        s["lacc"][...] += jnp.sum(t.reshape(64, 8, 256), axis=0)
        return 0

    pa.exchange()
    pb.exchange()
    lax.fori_loop(0, 16, loss_step, 0)
    loss_ref[...] = jnp.sum(s["lacc"][...], axis=0, keepdims=True)

    arrive(moved)
    for i in range(2):
        slot, src = where(table_ref[2 * own_n + i])
        for c in range(8):
            r0, l0 = 64 * i + 16 * (c // 2), 128 * (c % 2)
            wo_ref[r0:r0 + 16, l0:l0 + 128] = f(wall[src, slot, c])
            mo_ref[r0:r0 + 16, l0:l0 + 128] = f(s["mv_in"][c, i, 0:16])
            vo_ref[r0:r0 + 16, l0:l0 + 128] = f(s["mv_in"][c, i, 16:32])
    for made in pending[:-14]:
        made.wait_send()
    go_ref[:, 0:128] = pa.gradient()
    go_ref[:, 128:256] = pb.gradient()
    for made in pending[-14:]:
        made.wait_send()


def shards(
    tokens, queries, key_vectors, cotangent, positions, doc_ids, weight, moment_one, moment_two, old_ids, new_ids
):
    index = jnp.arange(64, dtype=jnp.int32)
    entry = jnp.arange(128, dtype=jnp.int32)
    table = jnp.sum(
        jnp.where(old_ids[None, :] == entry[:, None], index[None, :], 0)
        + jnp.where(index[None, :] + 64 == entry[:, None], new_ids[None, :], 0),
        axis=1,
    )
    lane = jnp.arange(256, dtype=jnp.int32)
    half = (lane % 32).astype(F32)
    frequency = rope_base ** (-(half * 2.0 / 64))
    angles = positions.astype(F32)[:, None] * frequency[None, :]
    signed = jnp.where((lane % 64) < 32, -jnp.sin(angles), jnp.sin(angles))
    trig = jnp.where(lane < 128, jnp.cos(angles), signed)
    small = jnp.concatenate([weight, moment_one, moment_two], axis=0)

    vmem = pl.BlockSpec(memory_space=pltpu.VMEM)
    smem = pl.BlockSpec(memory_space=pltpu.SMEM)
    outs = pl.pallas_call(
        kernel,
        out_shape=[jax.ShapeDtypeStruct((128, 256), F32)] * 4 + [jax.ShapeDtypeStruct((1, 256), F32)],
        in_specs=[smem] + [vmem] * 4 + [pl.BlockSpec(memory_space=pl.ANY)] * 3,
        out_specs=[vmem] * 5,
        scratch_shapes=list(PLAN.values()),
        compiler_params=pltpu.CompilerParams(
            collective_id=0, has_side_effects=True, vmem_limit_bytes=53760 * 1024
        ),
        cost_estimate=pl.CostEstimate(flops=2_200_000_000, bytes_accessed=6_000_000, transcendentals=2_200_000),
    )(table, trig, small, key_vectors, doc_ids.reshape(1, 256), queries, cotangent, tokens)
    return adam_step(*outs[:4]) + (outs[4].reshape(256),)


def solution(mesh):
    in_specs = (
        P(("rep", "fsdp"), None),
        P(("rep", "fsdp"), None),
        P(("rep", "fsdp"), None),
        P(("rep", "fsdp"), None),
        P(("rep", "fsdp")),
        P(("rep", "fsdp")),
        P("fsdp", None),
        P("fsdp", None),
        P("fsdp", None),
        P(),
        P(),
    )
    out_specs = (P("fsdp", None), P("fsdp", None), P("fsdp", None), P(("rep", "fsdp")))
    return jax.shard_map(shards, mesh=mesh, in_specs=in_specs, out_specs=out_specs, check_vma=False)
```
